1024 devices in a mesh: row: 64 (over y, x, core), col: 16 (over z).
Axes of the slice: x: 4, y: 8, z: 16, core: 2. Of those that a mesh axis runs over, the one named last changes fastest.
Arguments:
- user_factors: bfloat16 [131072, 256], P(('row', 'col')), may hold values from -0.375 to 0.375
- item_factors: float32 [262144, 256], P(('row', 'col')), may hold values from -4 to 4
- send_rows: int32 [65536, 16], P(('row', 'col')), may hold values from 0 to 127, as said below
- tile_users: int32 [8192, 128], P(('row', 'col')), may hold values from 0 to 1023
- tile_block: int32 [8192], P(('row', 'col')), may hold values from 0 to 1
- tile_counts: int32 [8192, 128, 128], P(('row', 'col')), may hold values from 0 to 7
- tile_live: int32 [64, 16], P('row', 'col'), may hold values from 4 to 8, as said below
Outputs:
- new_items: float32 [262144, 256], P(('row', 'col'))
The draws below stay inside these ranges and needn't reach their ends.
Inputs may be any that keep to these rules, and one draw needn't show every extreme that they name: `send_rows`: each row of a device's list for one destination holds distinct local user rows. `tile_live`: at least half of the slots are live; some device has all 8 live.
All inputs are finite; a program needn't handle non-finite values.
Results may differ from the reference program's by a relative error of at most 0.0007.
Values may be sent and summed in bfloat16 or wider, within the bound.
A program may use at most 32 MiB of HBM per device.

```python
import jax
import jax.numpy as jnp
from jax import lax

F = 256
BLOCK = 128
ITERS = 3
U_DEV = 128
IB_DEV = 2
TILES_DEV = 8
RP = 16
USERS = 131072
ITEMS = 262144
N_ROW = 64
N_COL = 16
DEVICES = 1024


def draw_send_rows(key, part):
    key = jax.random.fold_in(key, 11)
    keys = jax.random.split(key, DEVICES * N_ROW)
    picks = jax.vmap(lambda k: jax.random.permutation(k, U_DEV)[:RP])(keys)
    return picks.astype(jnp.int32)


def draw_tile_live(key, part):
    key = jax.random.fold_in(key, 23)
    first, second = jax.random.split(key)
    values = jax.random.randint(first, (N_ROW * N_COL,), TILES_DEV // 2, TILES_DEV + 1).astype(jnp.int32)
    where = jax.random.randint(second, (), 0, N_ROW * N_COL)
    values = values.at[where].set(TILES_DEV)
    return values.reshape(N_ROW, N_COL)


def with_ends(values, own_key, low, high):
    index_at = [jax.random.randint(jax.random.fold_in(own_key, axis), (), 0, length) for axis, length in enumerate(values.shape)]
    longest = values.shape.index(max(values.shape))
    beside = index_at[:longest] + [(index_at[longest] + 1) % values.shape[longest]] + index_at[longest + 1:]
    return values.at[tuple(index_at)].set(low).at[tuple(beside)].set(high)


def block_scale(rng, dims, cuts, least, largest):
    def one(position, shards_of):
        heights = jax.random.uniform(jax.random.fold_in(jax.random.fold_in(rng, 6), position), (shards_of,), jnp.float32, least / len(cuts), largest / len(cuts))
        return jnp.repeat(jnp.exp(heights), dims[position] // shards_of).reshape((-1,) + (1,) * (len(dims) - position - 1))

    level = one(*cuts[0])
    for cut in cuts[1:]:
        level = level * one(*cut)
    return level


def centred(rng, shape, deviation, limit, pieces=(), kind=jnp.bfloat16):
    array = deviation * jax.random.normal(rng, shape, jnp.float32)
    if pieces:
        array = array * block_scale(rng, shape, pieces, -0.22, 0.18)
    return jnp.clip(array, -limit, limit).astype(kind)


def setup_inputs(seed: int = 0) -> dict:
    seeds = jax.random.split(jax.random.key(seed), 8)
    user_factors = centred(seeds[0], (USERS, F), F ** -0.5, 0.375, ((0, 1024),))
    item_factors = centred(seeds[1], (ITEMS, F), 0.3, 4.0, ((0, 1024),), jnp.float32)
    send_rows = draw_send_rows(jax.random.fold_in(seeds[7], 71), 0)
    tile_users = with_ends(jax.random.randint(seeds[3], (DEVICES * TILES_DEV, BLOCK), 0, N_ROW * RP), jax.random.fold_in(seeds[3], 1), 0, (N_ROW * RP) - 1).astype(jnp.int32)
    tile_block = with_ends(jax.random.randint(seeds[4], (DEVICES * TILES_DEV,), 0, IB_DEV), jax.random.fold_in(seeds[4], 1), 0, IB_DEV - 1).astype(jnp.int32)
    tile_counts = with_ends(jax.random.randint(seeds[5], (DEVICES * TILES_DEV, BLOCK, BLOCK), 0, 8), jax.random.fold_in(seeds[5], 1), 0, 7).astype(jnp.int32)
    tile_live = draw_tile_live(jax.random.fold_in(seeds[7], 71), 0)
    return {"user_factors": user_factors, "item_factors": item_factors, "send_rows": send_rows, "tile_users": tile_users, "tile_block": tile_block, "tile_counts": tile_counts, "tile_live": tile_live}


HI = lax.Precision.HIGHEST


def item_solve(gram, recv, users_idx, blocks, counts, live, start):
    tiles = users_idx.shape[0]
    side = users_idx.shape[1]
    nblocks = start.shape[0] // side
    width = start.shape[1]
    tile_rows = recv[users_idx].astype(jnp.float32)
    alive = (jnp.arange(tiles, dtype=jnp.int32) < live).astype(jnp.float32)
    conf = 40.0 * counts.astype(jnp.float32) * alive[:, None, None]
    pref = (counts > 0).astype(jnp.float32) * alive[:, None, None]
    onehot = (blocks[:, None] == jnp.arange(nblocks, dtype=jnp.int32)[None, :]).astype(jnp.float32)

    def back(contrib):
        return jnp.einsum('tk,tif->kif', onehot, contrib, precision=HI).reshape(nblocks * side, width)

    def hessian(field):
        per_tile = jnp.einsum('tk,kif->tif', onehot, field.reshape(nblocks, side, width), precision=HI)
        scores = jnp.einsum('tif,tuf->tiu', per_tile, tile_rows, precision=HI)
        contrib = jnp.einsum('tiu,tuf->tif', conf * scores, tile_rows, precision=HI)
        return jnp.dot(field, gram, precision=HI) + 0.1 * field + back(contrib)

    rhs = back(jnp.einsum('tiu,tuf->tif', (1.0 + conf) * pref, tile_rows, precision=HI))
    solution = start
    resid = rhs - hessian(solution)
    direction = resid
    norm_now = jnp.sum(resid * resid, axis=1, keepdims=True)
    for step in range(ITERS):
        image = hessian(direction)
        alpha = norm_now / jnp.sum(direction * image, axis=1, keepdims=True)
        solution = solution + alpha * direction
        resid = resid - alpha * image
        norm_next = jnp.sum(resid * resid, axis=1, keepdims=True)
        direction = resid + (norm_next / norm_now) * direction
        norm_now = norm_next
    return solution


def reference(user_factors, item_factors, send_rows, tile_users, tile_block, tile_counts, tile_live):
    gram = jnp.dot(user_factors.T, user_factors, preferred_element_type=jnp.float32)
    lists = send_rows.reshape(DEVICES, N_ROW, RP)
    users_all = tile_users.reshape(DEVICES, TILES_DEV, BLOCK)
    blocks_all = tile_block.reshape(DEVICES, TILES_DEV)
    counts_all = tile_counts.reshape(DEVICES, TILES_DEV, BLOCK, BLOCK)
    live_all = tile_live.reshape(DEVICES)
    items_all = item_factors.reshape(DEVICES, IB_DEV * BLOCK, F)

    def one_device(dev):
        rowpos = dev // N_COL
        colpos = dev % N_COL
        sources = jnp.arange(N_ROW, dtype=jnp.int32) * N_COL + colpos
        chosen = lists[sources, rowpos]
        global_rows = sources[:, None] * U_DEV + chosen
        recv = user_factors[global_rows.reshape(-1)]
        return item_solve(gram, recv, users_all[dev], blocks_all[dev], counts_all[dev], live_all[dev], items_all[dev])

    result = lax.map(one_device, jnp.arange(DEVICES, dtype=jnp.int32))
    return result.reshape(ITEMS, F)
```

```python
import functools

import jax
import jax.numpy as jnp
from jax import lax
from jax.experimental import pallas as pl
from jax.experimental.pallas import tpu as pltpu
from jax.sharding import PartitionSpec as P

ITERS = 3
CORES_X = 8
MESH = pl.DeviceIdType.MESH
F32 = jnp.float32
BF16 = jnp.bfloat16

NN = (((1,), (0,)), ((), ()))
NT = (((1,), (1,)), ((), ()))
TN = (((0,), (0,)), ((), ()))


def dot(a, b, dims=NN):
    return lax.dot_general(a, b, dims, preferred_element_type=F32)


def split(x):
    high = x.astype(BF16)
    return high, (x - high.astype(F32)).astype(BF16)


def kernel(
    n_row, n_col, side,
    users_ref, items_ref, send_ref, tile_users_ref, tile_block_ref, counts_ref, live_ref,
    out_ref,
    outgoing, recv, local, s1, p1, s2, p2, s3, s4, full, hot, left, conf, rh, rl,
    row_send, row_recv, send_sems, recv_sems,
):
    r = lax.axis_index("row")
    c = lax.axis_index("col")
    nj = side
    ny = n_row // nj
    j = lax.rem(r, nj)
    y = lax.div(r, nj)
    tiles_j = s1.shape[1]
    tiles_y = s2.shape[1]
    rows_dev, width = users_ref.shape
    slots = send_ref.shape[1]
    n_recv = n_row * slots

    barrier = pltpu.get_barrier_semaphore()

    def greet_row(k, carry):
        pl.semaphore_signal(barrier, inc=1, device_id=(lax.rem(r + k, n_row), c), device_id_type=MESH)
        return carry

    def greet_col(k, carry):
        pl.semaphore_signal(barrier, inc=1, device_id=(r, lax.rem(c + k, n_col)), device_id_type=MESH)
        return carry

    lax.fori_loop(1, n_row, greet_row, 0)
    lax.fori_loop(1, n_col, greet_col, 0)

    u = users_ref[...]
    gram = dot(u, u, TN)
    for a in range(width // 8):
        for h in range(width // 128):
            local[a * (width // 128) + h] = gram[8 * a:8 * a + 8, 128 * h:128 * h + 128]

    wanted = send_ref[...][:, :, None]
    pick = (wanted == lax.broadcasted_iota(jnp.int32, (n_row, slots, rows_dev), 2)).astype(F32)
    rows_out = dot(pick.reshape(n_recv, rows_dev).astype(BF16), u).astype(BF16)
    outgoing[...] = rows_out.reshape(n_row, slots, width)

    pl.semaphore_wait(barrier, n_row - 1 + n_col - 1)

    def stage(index, count, source, target, device):
        def one(k, carry):
            pltpu.make_async_remote_copy(
                src_ref=source(k), dst_ref=target, send_sem=send_sems.at[index], recv_sem=recv_sems.at[index],
                device_id=device(k), device_id_type=MESH,
            ).start()
            return carry

        lax.fori_loop(1, count, one, 0)

    def arrived(index, buffer, count):
        view = buffer.at[pl.ds(0, count - 1)]
        pltpu.make_async_copy(view, view, recv_sems.at[index]).wait()

    def peer_j(k):
        return lax.rem(j + k, nj)

    def peer_y(k):
        return lax.rem(y + k, ny)

    def peer_z(k):
        return lax.rem(c + k, n_col)

    stage(0, nj, lambda k: local.at[pl.ds(peer_j(k) * tiles_j, tiles_j)], s1.at[j],
          lambda k: (y * nj + peer_j(k), c))

    def send_row(k, carry):
        peer = lax.rem(r + k, n_row)
        pltpu.make_async_remote_copy(
            src_ref=outgoing.at[peer], dst_ref=recv.at[r], send_sem=row_send, recv_sem=row_recv,
            device_id=(peer, c), device_id_type=MESH,
        ).start()
        return carry

    lax.fori_loop(1, n_row, send_row, 0)
    recv[r] = outgoing[r]
    s1[j] = local[pl.ds(j * tiles_j, tiles_j)]

    tiles = tile_users_ref.shape[0]
    block = tile_users_ref.shape[1]
    blocks = items_ref.shape[0] // block
    for t in range(tiles):
        row = tile_users_ref[t:t + 1, :]
        hit = lax.broadcasted_iota(jnp.int32, (n_recv, block), 0) == row
        hot[:, t * block:(t + 1) * block] = hit.astype(F32).astype(BF16)

    arrived(0, s1, nj)
    total = s1[0]
    for k in range(1, nj):
        total = total + s1[k]
    p1[...] = total

    stage(1, ny, lambda k: p1.at[pl.ds(peer_y(k) * tiles_y, tiles_y)], s2.at[y],
          lambda k: (peer_y(k) * nj + j, c))
    s2[y] = p1[pl.ds(y * tiles_y, tiles_y)]

    live = live_ref[0, 0]
    half = blocks * block
    for t in range(tiles):
        counts = counts_ref[t].astype(F32)
        pref = (counts > 0).astype(F32)
        alive = (t < live).astype(F32)
        for k in range(blocks):
            mine = (tile_block_ref[t] == k).astype(F32) * alive
            left[k * block:(k + 1) * block, t * block:(t + 1) * block] = (counts * mine).astype(BF16)
            left[half + k * block:half + (k + 1) * block, t * block:(t + 1) * block] = (pref * mine).astype(BF16)

    arrived(1, s2, ny)
    total = s2[0]
    for k in range(1, ny):
        total = total + s2[k]
    p2[...] = total

    stage(2, n_col, lambda k: p2, s3.at[c], lambda k: (r, peer_z(k)))
    s3[c] = p2[...]

    sums = dot(left[...], hot[...], NT)
    conf_all = 40.0 * sums[:half]
    conf[...] = conf_all
    high, low = split(sums[half:] + conf_all)
    rh[...] = high
    rl[...] = low

    arrived(2, s3, n_col)
    total = s3[0]
    for k in range(1, n_col):
        total = total + s3[k]
    s4[y] = total

    stage(3, ny, lambda k: s4.at[y], s4.at[y], lambda k: (peer_y(k) * nj + j, c))
    arrived(3, s4, ny)

    stage(4, nj, lambda k: s4, full.at[j], lambda k: (y * nj + peer_j(k), c))
    full[j] = s4[...]

    view = recv.at[pl.ds(0, n_row - 1)]
    pltpu.make_async_copy(view, view, row_recv).wait()

    rows = recv[...].reshape(n_recv, width)

    def tile_part(parts):
        vh, vl = parts
        scores = dot(vh, rows, NT) + dot(vl, rows, NT)
        wh, wl = split(conf[...] * scores)
        return dot(wh, rows) + dot(wl, rows)

    start = items_ref[...]
    parts = split(start)
    resid = dot(rh[...], rows) + dot(rl[...], rows) - tile_part(parts) - 0.1 * start

    arrived(4, full, nj)
    strips = []
    per = width // 128
    for a in range(width // 8):
        cells = [full[(a * per + h) // tiles_j, ((a * per + h) % tiles_j) // tiles_y, (a * per + h) % tiles_y] for h in range(per)]
        strips.append(jnp.concatenate(cells, axis=1))
    gh, gl = split(jnp.concatenate(strips, axis=0))

    def gram_part(parts):
        vh, vl = parts
        return dot(vh, gh) + dot(vl, gh) + dot(vh, gl)

    resid = resid - gram_part(parts)
    solution = start
    direction = resid
    norm_now = jnp.sum(resid * resid, axis=1, keepdims=True)
    for step in range(ITERS):
        parts = split(direction)
        image = tile_part(parts) + gram_part(parts) + 0.1 * direction
        alpha = norm_now / jnp.sum(direction * image, axis=1, keepdims=True)
        solution = solution + alpha * direction
        if step < ITERS - 1:
            resid = resid - alpha * image
            norm_next = jnp.sum(resid * resid, axis=1, keepdims=True)
            direction = resid + norm_next / norm_now * direction
            norm_now = norm_next
    out_ref[...] = solution

    view = outgoing.at[pl.ds(0, n_row - 1)]
    pltpu.make_async_copy(view, view, row_send).wait()
    for index, (buffer, count) in enumerate(((s1, nj), (s2, ny), (s3, n_col), (s4, ny), (full, nj))):
        view = buffer.at[pl.ds(0, count - 1)]
        pltpu.make_async_copy(view, view, send_sems.at[index]).wait()


def body(n_row, n_col, side, user_factors, item_factors, send_rows, tile_users, tile_block, tile_counts, tile_live):
    rows_dev, width = user_factors.shape
    slots = send_rows.shape[1]
    ny = n_row // side
    n_tiles = width // 8 * (width // 128)
    tiles_j = n_tiles // side
    tiles_y = tiles_j // ny
    n_recv = n_row * slots
    columns = tile_users.shape[0] * tile_users.shape[1]
    items = item_factors.shape[0]
    vmem = pl.BlockSpec(memory_space=pltpu.VMEM)
    smem = pl.BlockSpec(memory_space=pltpu.SMEM)
    return pl.pallas_call(
        functools.partial(kernel, n_row, n_col, side),
        out_shape=jax.ShapeDtypeStruct(item_factors.shape, F32),
        in_specs=[vmem, vmem, vmem, vmem, smem, vmem, smem],
        out_specs=vmem,
        scratch_shapes=[
            pltpu.VMEM((n_row, slots, width), BF16),
            pltpu.VMEM((n_row, slots, width), BF16),
            pltpu.VMEM((n_tiles, 8, 128), F32),
            pltpu.VMEM((side, tiles_j, 8, 128), F32),
            pltpu.VMEM((tiles_j, 8, 128), F32),
            pltpu.VMEM((ny, tiles_y, 8, 128), F32),
            pltpu.VMEM((tiles_y, 8, 128), F32),
            pltpu.VMEM((n_col, tiles_y, 8, 128), F32),
            pltpu.VMEM((ny, tiles_y, 8, 128), F32),
            pltpu.VMEM((side, ny, tiles_y, 8, 128), F32),
            pltpu.VMEM((n_recv, columns), BF16),
            pltpu.VMEM((2 * items, columns), BF16),
            pltpu.VMEM((items, n_recv), F32),
            pltpu.VMEM((items, n_recv), BF16),
            pltpu.VMEM((items, n_recv), BF16),
            pltpu.SemaphoreType.DMA,
            pltpu.SemaphoreType.DMA,
            pltpu.SemaphoreType.DMA((5,)),
            pltpu.SemaphoreType.DMA((5,)),
        ],
        compiler_params=pltpu.CompilerParams(
            collective_id=0, has_side_effects=True, vmem_limit_bytes=48 * 1024 * 1024
        ),
    )(user_factors, item_factors, send_rows, tile_users, tile_block, tile_counts, tile_live)


def solution(mesh):
    n_row, n_col = mesh.shape["row"], mesh.shape["col"]
    in_specs = (
        P(("row", "col"), None),
        P(("row", "col"), None),
        P(("row", "col"), None),
        P(("row", "col"), None),
        P(("row", "col")),
        P(("row", "col"), None, None),
        P("row", "col"),
    )
    return jax.shard_map(
        functools.partial(body, n_row, n_col, min(CORES_X, n_row // 2)),
        mesh=mesh, in_specs=in_specs, out_specs=P(("row", "col"), None), check_vma=False,
    )
```

```python
import functools

import jax
import jax.numpy as jnp
from jax import lax
from jax.experimental import pallas as pl
from jax.experimental.pallas import tpu as pltpu
from jax.sharding import PartitionSpec as P

ITERS = 3
MESH = pl.DeviceIdType.MESH
F32 = jnp.float32
BF16 = jnp.bfloat16

NN = (((1,), (0,)), ((), ()))
NT = (((1,), (1,)), ((), ()))
TN = (((0,), (0,)), ((), ()))


def dot(a, b, dims=NN):
    return lax.dot_general(a, b, dims, preferred_element_type=F32)


def split(x):
    high = x.astype(BF16)
    return high, (x - high.astype(F32)).astype(BF16)


def far_first(n):
    return sorted(range(1, n), key=lambda k: -min(k, n - k))


def kernel(
    dims,
    users_hbm, items_hbm, wanted_hbm, tile_users_hbm, tile_block_hbm, counts_hbm, live_hbm,
    out_ref,
    users_ref, items_ref, wanted_ref, tile_users_ref, tile_block_ref, counts_ref, live_ref,
    outgoing, recv, local, s0, p0, s1, p1, s2, p2, s3, s4, full, hot, left, conf, rh, rl,
    load_sems, row_send, row_recv, send_sems, recv_sems,
):
    ny, nx, n_col = dims
    n_row = ny * nx * 2
    r = lax.axis_index("row")
    c = lax.axis_index("col")
    core = lax.rem(r, 2)
    x = lax.rem(lax.div(r, 2), nx)
    y = lax.div(r, 2 * nx)
    rows_dev, width = users_ref.shape
    slots = wanted_ref.shape[0]
    n_recv = n_row * slots

    barrier = pltpu.get_barrier_semaphore()
    for k in far_first(n_col):
        pl.semaphore_signal(barrier, inc=1, device_id=(r, lax.rem(c + k, n_col)), device_id_type=MESH)

    def greet_row(k, carry):
        pl.semaphore_signal(barrier, inc=1, device_id=(lax.rem(r + k, n_row), c), device_id_type=MESH)
        return carry

    loads = [
        pltpu.make_async_copy(source, target, load_sems.at[i])
        for i, (source, target) in enumerate((
            (users_hbm, users_ref), (wanted_hbm, wanted_ref), (items_hbm, items_ref), (tile_users_hbm, tile_users_ref),
            (tile_block_hbm, tile_block_ref), (live_hbm, live_ref), (counts_hbm, counts_ref),
        ))
    ]
    for load in loads:
        load.start()
    lax.fori_loop(1, n_row, greet_row, 0)
    loads[0].wait()
    loads[1].wait()

    per = width // 128
    u = users_ref[...]
    gram = dot(u, u, TN)
    for a in range(width // 8):
        for h in range(per):
            local[a * per + h] = gram[8 * a:8 * a + 8, 128 * h:128 * h + 128]

    wanted = wanted_ref[...].T[:, :, None]
    pick = (wanted == lax.broadcasted_iota(jnp.int32, (n_row, slots, rows_dev), 2)).astype(F32)
    rows_out = dot(pick.reshape(n_recv, rows_dev).astype(BF16), u).astype(BF16)
    outgoing[...] = rows_out.reshape(n_row, slots, width)

    pl.semaphore_wait(barrier, n_row - 1 + n_col - 1)

    def send(index, source, target, device):
        pltpu.make_async_remote_copy(
            src_ref=source, dst_ref=target, send_sem=send_sems.at[index], recv_sem=recv_sems.at[index],
            device_id=device, device_id_type=MESH,
        ).start()

    def wait(view, sem):
        pltpu.make_async_copy(view, view, sem).wait()

    def arrived(index, view):
        wait(view, recv_sems.at[index])

    def total(buffer, count):
        value = buffer[0]
        for k in range(1, count):
            value = value + buffer[k]
        return value

    def at(px, py, pcore):
        return ((py * nx + px) * 2 + pcore, c)

    def send_row(k, carry):
        peer = lax.rem(r + k, n_row)
        pltpu.make_async_remote_copy(
            src_ref=outgoing.at[peer], dst_ref=recv.at[r], send_sem=row_send, recv_sem=row_recv,
            device_id=(peer, c), device_id_type=MESH,
        ).start()
        return carry

    def send_rows():
        lax.fori_loop(1, n_row, send_row, 0)

    half_tiles = s0.shape[0]
    send(0, local.at[pl.ds((1 - core) * half_tiles, half_tiles)], s0, at(x, y, 1 - core))
    recv[r] = outgoing[r]
    arrived(0, s0)
    p0[...] = local[pl.ds(core * half_tiles, half_tiles)] + s0[...]

    tiles_x = s1.shape[1]
    for k in far_first(nx):
        px = lax.rem(x + k, nx)
        send(1, p0.at[pl.ds(px * tiles_x, tiles_x)], s1.at[x], at(px, y, core))
    s1[x] = p0[pl.ds(x * tiles_x, tiles_x)]
    arrived(1, s1.at[pl.ds(0, nx - 1)])
    p1[...] = total(s1, nx)

    tiles_y = s2.shape[1]
    for k in far_first(ny):
        py = lax.rem(y + k, ny)
        send(2, p1.at[pl.ds(py * tiles_y, tiles_y)], s2.at[y], at(x, py, core))
    s2[y] = p1[pl.ds(y * tiles_y, tiles_y)]
    arrived(2, s2.at[pl.ds(0, ny - 1)])
    p2[...] = total(s2, ny)

    for k in far_first(n_col):
        send(3, p2, s3.at[c], (r, lax.rem(c + k, n_col)))
    s3[c] = p2[...]
    send_rows()

    for load in loads[2:]:
        load.wait()
    tiles = tile_users_ref.shape[0]
    block = tile_users_ref.shape[1]
    blocks = items_ref.shape[0] // block
    items = blocks * block
    live = live_ref[0, 0]
    for t in range(tiles):
        columns = slice(t * block, (t + 1) * block)
        hit = lax.broadcasted_iota(jnp.int32, (n_recv, block), 0) == tile_users_ref[t:t + 1, :]
        hot[:, columns] = hit.astype(F32).astype(BF16)
        counts = counts_ref[t].astype(F32)
        pref = (counts > 0).astype(F32)
        alive = (t < live).astype(F32)
        for k in range(blocks):
            mine = (tile_block_ref[t] == k).astype(F32) * alive
            left[k * block:(k + 1) * block, columns] = (counts * mine).astype(BF16)
            left[items + k * block:items + (k + 1) * block, columns] = (pref * mine).astype(BF16)
    sums = dot(left[...], hot[...], NT)
    conf_all = 40.0 * sums[:items]
    conf[...] = conf_all
    high, low = split(sums[items:] + conf_all)
    rh[...] = high
    rl[...] = low

    arrived(3, s3.at[pl.ds(0, n_col - 1)])
    s4[y] = total(s3, n_col)

    for k in far_first(ny):
        send(4, s4.at[y], s4.at[y], at(x, lax.rem(y + k, ny), core))
    arrived(4, s4.at[pl.ds(0, ny - 1)])

    for k in far_first(nx):
        send(5, s4, full.at[core, x], at(lax.rem(x + k, nx), y, core))
    full[core, x] = s4[...]

    wait(recv.at[pl.ds(0, n_row - 1)], row_recv)
    arrived(5, full.at[0, pl.ds(0, nx - 1)])

    send(6, full.at[core], full.at[core], at(x, y, 1 - core))

    rows = recv[...].reshape(n_recv, width)

    def tile_part(parts):
        vh, vl = parts
        scores = dot(vh, rows, NT) + dot(vl, rows, NT)
        wh, wl = split(conf[...] * scores)
        return dot(wh, rows) + dot(wl, rows)

    start = items_ref[...]
    parts = split(start)
    resid = dot(rh[...], rows) + dot(rl[...], rows) - tile_part(parts) - 0.1 * start

    arrived(6, full.at[0])
    strips = []
    for a in range(width // 8):
        cells = []
        for h in range(per):
            t = a * per + h
            cells.append(full[t // half_tiles, t % half_tiles // tiles_x, t % tiles_x // tiles_y, t % tiles_y])
        strips.append(jnp.concatenate(cells, axis=1))
    gh, gl = split(jnp.concatenate(strips, axis=0))

    def gram_part(parts):
        vh, vl = parts
        return dot(vh, gh) + dot(vl, gh) + dot(vh, gl)

    resid = resid - gram_part(parts)
    solution = start
    direction = resid
    norm_now = jnp.sum(resid * resid, axis=1, keepdims=True)
    for step in range(ITERS):
        parts = split(direction)
        image = tile_part(parts) + gram_part(parts) + 0.1 * direction
        alpha = norm_now / jnp.sum(direction * image, axis=1, keepdims=True)
        solution = solution + alpha * direction
        if step < ITERS - 1:
            resid = resid - alpha * image
            norm_next = jnp.sum(resid * resid, axis=1, keepdims=True)
            direction = resid + norm_next / norm_now * direction
            norm_now = norm_next
    out_ref[...] = solution

    wait(outgoing.at[pl.ds(0, n_row - 1)], row_send)
    sent = (s0, s1.at[pl.ds(0, nx - 1)], s2.at[pl.ds(0, ny - 1)], s3.at[pl.ds(0, n_col - 1)], s4.at[pl.ds(0, ny - 1)],
            full.at[0, pl.ds(0, nx - 1)], full.at[0])
    for index, view in enumerate(sent):
        wait(view, send_sems.at[index])

def body(dims, user_factors, item_factors, send_rows, tile_users, tile_block, tile_counts, tile_live):
    ny, nx, n_col = dims
    n_row = ny * nx * 2
    width = user_factors.shape[1]
    slots = send_rows.shape[1]
    n_tiles = width // 8 * (width // 128)
    tiles_x = n_tiles // 2 // nx
    tiles_y = tiles_x // ny
    n_recv = n_row * slots
    columns = tile_users.shape[0] * tile_users.shape[1]
    items = item_factors.shape[0]
    operands = (user_factors, item_factors, send_rows.T, tile_users, tile_block, tile_counts, tile_live)
    places = (pltpu.VMEM, pltpu.VMEM, pltpu.VMEM, pltpu.VMEM, pltpu.SMEM, pltpu.VMEM, pltpu.SMEM)

    def cells(*lead):
        return pltpu.VMEM((*lead, 8, 128), F32)

    return pl.pallas_call(
        functools.partial(kernel, dims),
        out_shape=jax.ShapeDtypeStruct(item_factors.shape, F32),
        in_specs=[pl.BlockSpec(memory_space=pltpu.HBM)] * len(operands),
        out_specs=pl.BlockSpec(memory_space=pltpu.VMEM),
        scratch_shapes=[place(a.shape, a.dtype) for place, a in zip(places, operands)] + [
            pltpu.VMEM((n_row, slots, width), BF16),
            pltpu.VMEM((n_row, slots, width), BF16),
            cells(n_tiles),
            cells(n_tiles // 2),
            cells(n_tiles // 2),
            cells(nx, tiles_x),
            cells(tiles_x),
            cells(ny, tiles_y),
            cells(tiles_y),
            cells(n_col, tiles_y),
            cells(ny, tiles_y),
            cells(2, nx, ny, tiles_y),
            pltpu.VMEM((n_recv, columns), BF16),
            pltpu.VMEM((2 * items, columns), BF16),
            pltpu.VMEM((items, n_recv), F32),
            pltpu.VMEM((items, n_recv), BF16),
            pltpu.VMEM((items, n_recv), BF16),
            pltpu.SemaphoreType.DMA((len(operands),)),
            pltpu.SemaphoreType.DMA,
            pltpu.SemaphoreType.DMA,
            pltpu.SemaphoreType.DMA((7,)),
            pltpu.SemaphoreType.DMA((7,)),
        ],
        compiler_params=pltpu.CompilerParams(
            collective_id=0, has_side_effects=True, vmem_limit_bytes=58 * 1024 * 1024
        ),
    )(*operands)


def solution(mesh):
    n_row, n_col = mesh.shape["row"], mesh.shape["col"]
    nx = min(4, n_row // 4)
    in_specs = (
        P(("row", "col"), None),
        P(("row", "col"), None),
        P(("row", "col"), None),
        P(("row", "col"), None),
        P(("row", "col")),
        P(("row", "col"), None, None),
        P("row", "col"),
    )
    return jax.shard_map(
        functools.partial(body, (n_row // 2 // nx, nx, n_col)),
        mesh=mesh, in_specs=in_specs, out_specs=P(("row", "col"), None), check_vma=False,
    )
```

```python
import functools

import jax
import jax.numpy as jnp
from jax import lax
from jax.experimental import pallas as pl
from jax.experimental.pallas import tpu as pltpu
from jax.sharding import PartitionSpec as P

ITERS = 3
FIRST = (4, 3, 5)
MESH = pl.DeviceIdType.MESH
F32 = jnp.float32
BF16 = jnp.bfloat16

NN = (((1,), (0,)), ((), ()))
NT = (((1,), (1,)), ((), ()))
TN = (((0,), (0,)), ((), ()))


def dot(a, b, dims=NN):
    return lax.dot_general(a, b, dims, preferred_element_type=F32)


def split(x):
    high = x.astype(BF16)
    return high, (x - high.astype(F32)).astype(BF16)


def far_first(n):
    return sorted(range(1, n), key=lambda k: -min(k, n - k))


def near(n):
    return sorted({k % n for k in (2, -2, 1, -1)} - {0})


def parted(n):
    first = [k for k in FIRST if k < n]
    return first, [k for k in far_first(n) if k not in first]


def rounds(n):
    known, steps = 2, []
    while known < n // 2:
        steps.append(known)
        known *= 2
    return steps


def kernel(
    dims,
    users_hbm, items_hbm, wanted_hbm, tile_users_hbm, tile_block_hbm, counts_hbm, live_hbm,
    out_ref,
    users_ref, items_ref, wanted_ref, tile_users_ref, tile_block_ref, counts_ref, live_ref,
    outgoing, recv, local, s0, p0, s1, p1, s2, p2, s3, s4, full, hot, left, conf, rh, rl,
    load_sems, row_send, row_recv, send_sems, recv_sems, met_y, met_z,
):
    ny, nx, n_col = dims
    n_row = ny * nx * 2
    r = lax.axis_index("row")
    c = lax.axis_index("col")
    core = lax.rem(r, 2)
    x = lax.rem(lax.div(r, 2), nx)
    y = lax.div(r, 2 * nx)
    rows_dev, width = users_ref.shape
    slots = wanted_ref.shape[0]
    n_recv = n_row * slots

    def at(px, py, pcore):
        return ((py * nx + px) * 2 + pcore, c)

    def along_x(k):
        return at(lax.rem(x + k, nx), y, core)

    def along_y(k):
        return at(x, lax.rem(y + k, ny), core)

    def along_z(k):
        return (r, lax.rem(c + k, n_col))

    barrier = pltpu.get_barrier_semaphore()
    friends = [at(x, y, 1 - core)] + [along_x(k) for k in range(1, nx)]
    friends += [along_y(k) for k in near(ny)] + [along_z(k) for k in near(n_col)]
    for friend in friends:
        pl.semaphore_signal(barrier, inc=1, device_id=friend, device_id_type=MESH)

    loads = [
        pltpu.make_async_copy(source, target, load_sems.at[i])
        for i, (source, target) in enumerate((
            (users_hbm, users_ref), (wanted_hbm, wanted_ref), (items_hbm, items_ref), (tile_users_hbm, tile_users_ref),
            (tile_block_hbm, tile_block_ref), (live_hbm, live_ref), (counts_hbm, counts_ref),
        ))
    ]
    for load in loads:
        load.start()
    loads[0].wait()

    per = width // 128
    u = users_ref[...]
    gram = dot(u, u, TN)
    for a in range(width // 8):
        for h in range(per):
            local[a * per + h] = gram[8 * a:8 * a + 8, 128 * h:128 * h + 128]

    pl.semaphore_wait(barrier, len(friends))

    def meet(semaphores, i, n, along):
        for k in (rounds(n)[i], n - rounds(n)[i]):
            pl.semaphore_signal(semaphores.at[i], inc=1, device_id=along(k), device_id_type=MESH)

    def met(semaphores, i):
        pl.semaphore_wait(semaphores.at[i], 2)

    def send(index, source, target, device):
        pltpu.make_async_remote_copy(
            src_ref=source, dst_ref=target, send_sem=send_sems.at[index], recv_sem=recv_sems.at[index],
            device_id=device, device_id_type=MESH,
        ).start()

    def wait(view, sem):
        pltpu.make_async_copy(view, view, sem).wait()

    def arrived(index, view):
        wait(view, recv_sems.at[index])

    def total(buffer, count):
        value = buffer[0]
        for k in range(1, count):
            value = value + buffer[k]
        return value

    def send_rows(steps):
        side = 2 * nx
        for step in steps:
            def one(k, carry):
                peer = lax.rem(y + step, ny) * side + lax.rem(lax.rem(r, side) + k, side)
                pltpu.make_async_remote_copy(
                    src_ref=outgoing.at[peer], dst_ref=recv.at[r], send_sem=row_send, recv_sem=row_recv,
                    device_id=(peer, c), device_id_type=MESH,
                ).start()
                return carry

            lax.fori_loop(0 if step else 1, side, one, 0)

    first, second = parted(ny)

    half_tiles = s0.shape[0]
    send(0, local.at[pl.ds((1 - core) * half_tiles, half_tiles)], s0, at(x, y, 1 - core))
    if rounds(ny):
        meet(met_y, 0, ny, along_y)
    if rounds(n_col):
        meet(met_z, 0, n_col, along_z)
    arrived(0, s0)
    p0[...] = local[pl.ds(core * half_tiles, half_tiles)] + s0[...]

    tiles_x = s1.shape[1]
    for k in far_first(nx):
        px = lax.rem(x + k, nx)
        send(1, p0.at[pl.ds(px * tiles_x, tiles_x)], s1.at[x], along_x(k))
    s1[x] = p0[pl.ds(x * tiles_x, tiles_x)]
    for i in range(1, len(rounds(n_col))):
        met(met_z, i - 1)
        meet(met_z, i, n_col, along_z)
    arrived(1, s1.at[pl.ds(0, nx - 1)])
    p1[...] = total(s1, nx)

    if rounds(ny):
        met(met_y, 0)
    tiles_y = s2.shape[1]
    for k in far_first(ny):
        py = lax.rem(y + k, ny)
        send(2, p1.at[pl.ds(py * tiles_y, tiles_y)], s2.at[y], along_y(k))
    s2[y] = p1[pl.ds(y * tiles_y, tiles_y)]
    loads[1].wait()
    wanted = wanted_ref[...].T[:, :, None]
    pick = (wanted == lax.broadcasted_iota(jnp.int32, (n_row, slots, rows_dev), 2)).astype(F32)
    rows_out = dot(pick.reshape(n_recv, rows_dev).astype(BF16), u).astype(BF16)
    outgoing[...] = rows_out.reshape(n_row, slots, width)
    recv[r] = outgoing[r]
    send_rows([0])
    arrived(2, s2.at[pl.ds(0, ny - 1)])
    p2[...] = total(s2, ny)

    if rounds(n_col):
        met(met_z, len(rounds(n_col)) - 1)
    for k in far_first(n_col):
        send(3, p2, s3.at[c], along_z(k))
    s3[c] = p2[...]
    send_rows(first)

    for load in loads[2:]:
        load.wait()
    tiles = tile_users_ref.shape[0]
    block = tile_users_ref.shape[1]
    blocks = items_ref.shape[0] // block
    items = blocks * block
    live = live_ref[0]
    for t in range(tiles):
        columns = slice(t * block, (t + 1) * block)
        hit = lax.broadcasted_iota(jnp.int32, (n_recv, block), 0) == tile_users_ref[t:t + 1, :]
        hot[:, columns] = hit.astype(F32).astype(BF16)
        counts = counts_ref[t].astype(F32)
        pref = (counts > 0).astype(F32)
        alive = (t < live).astype(F32)
        for k in range(blocks):
            mine = (tile_block_ref[t] == k).astype(F32) * alive
            left[k * block:(k + 1) * block, columns] = (counts * mine).astype(BF16)
            left[items + k * block:items + (k + 1) * block, columns] = (pref * mine).astype(BF16)
    sums = dot(left[...], hot[...], NT)
    conf_all = 40.0 * sums[:items]
    conf[...] = conf_all
    high, low = split(sums[items:] + conf_all)
    rh[...] = high
    rl[...] = low

    arrived(3, s3.at[pl.ds(0, n_col - 1)])
    s4[y] = total(s3, n_col)

    for k in far_first(ny):
        send(4, s4.at[y], s4.at[y], along_y(k))
    send_rows(second)
    arrived(4, s4.at[pl.ds(0, ny - 1)])

    for k in far_first(nx):
        send(5, s4, full.at[core, x], along_x(k))
    full[core, x] = s4[...]

    arrived(5, full.at[0, pl.ds(0, nx - 1)])

    send(6, full.at[core], full.at[core], at(x, y, 1 - core))

    wait(recv.at[pl.ds(0, n_row - 1)], row_recv)

    rows = recv[...].reshape(n_recv, width)

    def tile_part(parts):
        vh, vl = parts
        scores = dot(vh, rows, NT) + dot(vl, rows, NT)
        wh, wl = split(conf[...] * scores)
        return dot(wh, rows) + dot(wl, rows)

    start = items_ref[...]
    parts = split(start)
    resid = dot(rh[...], rows) + dot(rl[...], rows) - tile_part(parts) - 0.1 * start

    arrived(6, full.at[0])
    strips = []
    for a in range(width // 8):
        cells = []
        for h in range(per):
            t = a * per + h
            cells.append(full[t // half_tiles, t % half_tiles // tiles_x, t % tiles_x // tiles_y, t % tiles_y])
        strips.append(jnp.concatenate(cells, axis=1))
    gh, gl = split(jnp.concatenate(strips, axis=0))

    def gram_part(parts):
        vh, vl = parts
        return dot(vh, gh) + dot(vl, gh) + dot(vh, gl)

    resid = resid - gram_part(parts)
    solution = start
    direction = resid
    norm_now = jnp.sum(resid * resid, axis=1, keepdims=True)
    for step in range(ITERS):
        parts = split(direction)
        image = tile_part(parts) + gram_part(parts) + 0.1 * direction
        alpha = norm_now / jnp.sum(direction * image, axis=1, keepdims=True)
        solution = solution + alpha * direction
        if step < ITERS - 1:
            resid = resid - alpha * image
            norm_next = jnp.sum(resid * resid, axis=1, keepdims=True)
            direction = resid + norm_next / norm_now * direction
            norm_now = norm_next
    out_ref[...] = solution

    wait(outgoing.at[pl.ds(0, n_row - 1)], row_send)
    sent = (s0, s1.at[pl.ds(0, nx - 1)], s2.at[pl.ds(0, ny - 1)], s3.at[pl.ds(0, n_col - 1)], s4.at[pl.ds(0, ny - 1)],
            full.at[0, pl.ds(0, nx - 1)], full.at[0])
    for index, view in enumerate(sent):
        wait(view, send_sems.at[index])

def body(dims, user_factors, item_factors, send_rows, tile_users, tile_block, tile_counts, tile_live):
    ny, nx, n_col = dims
    n_row = ny * nx * 2
    width = user_factors.shape[1]
    slots = send_rows.shape[1]
    n_tiles = width // 8 * (width // 128)
    tiles_x = n_tiles // 2 // nx
    tiles_y = tiles_x // ny
    n_recv = n_row * slots
    columns = tile_users.shape[0] * tile_users.shape[1]
    items = item_factors.shape[0]
    operands = (user_factors, item_factors, send_rows.T, tile_users, tile_block, tile_counts, tile_live.reshape(1))
    places = (pltpu.VMEM, pltpu.VMEM, pltpu.VMEM, pltpu.VMEM, pltpu.SMEM, pltpu.VMEM, pltpu.SMEM)

    def cells(*lead):
        return pltpu.VMEM((*lead, 8, 128), F32)

    return pl.pallas_call(
        functools.partial(kernel, dims),
        out_shape=pltpu.VMEM(item_factors.shape, F32),
        in_specs=[pl.BlockSpec(memory_space=pltpu.HBM)] * len(operands),
        out_specs=pl.BlockSpec(memory_space=pltpu.VMEM),
        scratch_shapes=[place(a.shape, a.dtype) for place, a in zip(places, operands)] + [
            pltpu.VMEM((n_row, slots, width), BF16),
            pltpu.VMEM((n_row, slots, width), BF16),
            cells(n_tiles),
            cells(n_tiles // 2),
            cells(n_tiles // 2),
            cells(nx, tiles_x),
            cells(tiles_x),
            cells(ny, tiles_y),
            cells(tiles_y),
            cells(n_col, tiles_y),
            cells(ny, tiles_y),
            cells(2, nx, ny, tiles_y),
            pltpu.VMEM((n_recv, columns), BF16),
            pltpu.VMEM((2 * items, columns), BF16),
            pltpu.VMEM((items, n_recv), F32),
            pltpu.VMEM((items, n_recv), BF16),
            pltpu.VMEM((items, n_recv), BF16),
            pltpu.SemaphoreType.DMA((len(operands),)),
            pltpu.SemaphoreType.DMA,
            pltpu.SemaphoreType.DMA,
            pltpu.SemaphoreType.DMA((7,)),
            pltpu.SemaphoreType.DMA((7,)),
            pltpu.SemaphoreType.REGULAR((max(1, len(rounds(ny))),)),
            pltpu.SemaphoreType.REGULAR((max(1, len(rounds(n_col))),)),
        ],
        compiler_params=pltpu.CompilerParams(
            collective_id=0, has_side_effects=True, vmem_limit_bytes=58 * 1024 * 1024
        ),
    )(*operands)


def solution(mesh):
    n_row, n_col = mesh.shape["row"], mesh.shape["col"]
    nx = min(4, n_row // 4)
    in_specs = (
        P(("row", "col"), None),
        P(("row", "col"), None),
        P(("row", "col"), None),
        P(("row", "col"), None),
        P(("row", "col")),
        P(("row", "col"), None, None),
        P("row", "col"),
    )
    return jax.shard_map(
        functools.partial(body, (n_row // 2 // nx, nx, n_col)),
        mesh=mesh, in_specs=in_specs, out_specs=P(("row", "col"), None), check_vma=False,
    )
```

```python
import functools

import jax
import jax.numpy as jnp
from jax import lax
from jax.experimental import pallas as pl
from jax.experimental.pallas import tpu as pltpu
from jax.sharding import PartitionSpec as P

ITERS = 3
FIRST = (4, 3, 5)
CHUNKS = 4
MESH = pl.DeviceIdType.MESH
F32 = jnp.float32
BF16 = jnp.bfloat16

NN = (((1,), (0,)), ((), ()))
NT = (((1,), (1,)), ((), ()))
TN = (((0,), (0,)), ((), ()))


def dot(a, b, dims=NN):
    return lax.dot_general(a, b, dims, preferred_element_type=F32)


def split(x):
    high = x.astype(BF16)
    return high, (x - high.astype(F32)).astype(BF16)


def stacked(x):
    return jnp.concatenate(split(x), axis=0)


def dot_stacked(parts, b, dims=NN):
    both = dot(parts, b, dims)
    half = both.shape[0] // 2
    return both[:half] + both[half:]


def far_first(n):
    return sorted(range(1, n), key=lambda k: -min(k, n - k))


def near(n):
    return sorted({k % n for k in (2, -2, 1, -1)} - {0})


def parted(n):
    first = [k for k in FIRST if k < n]
    return first, [k for k in far_first(n) if k not in first]


def rounds(n):
    known, steps = 2, []
    while known < n // 2:
        steps.append(known)
        known *= 2
    return steps


def kernel(
    dims,
    users_hbm, items_hbm, wanted_hbm, tile_users_hbm, tile_block_hbm, counts_hbm, live_hbm,
    out_ref,
    users_ref, items_ref, wanted_ref, tile_users_ref, tile_block_ref, counts_ref, live_ref,
    outgoing, recv, local, s0, p0, s1, p1, s2, p2, s3, s4, full, hot, left, conf, rh, rl,
    load_sems, row_send, row_recv, send_sems, recv_sems, met_y, met_z,
):
    ny, nx, n_col = dims
    n_row = ny * nx * 2
    r = lax.axis_index("row")
    c = lax.axis_index("col")
    core = lax.rem(r, 2)
    x = lax.rem(lax.div(r, 2), nx)
    y = lax.div(r, 2 * nx)
    rows_dev, width = users_ref.shape
    slots = wanted_ref.shape[0]
    n_recv = n_row * slots

    def at(px, py, pcore):
        return ((py * nx + px) * 2 + pcore, c)

    def along_x(k):
        return at(lax.rem(x + k, nx), y, core)

    def along_y(k):
        return at(x, lax.rem(y + k, ny), core)

    def along_z(k):
        return (r, lax.rem(c + k, n_col))

    loads = [
        pltpu.make_async_copy(source, target, load_sems.at[i])
        for i, (source, target) in enumerate((
            (users_hbm, users_ref), (wanted_hbm, wanted_ref), (items_hbm, items_ref), (tile_users_hbm, tile_users_ref),
            (tile_block_hbm, tile_block_ref), (live_hbm, live_ref), (counts_hbm, counts_ref),
        ))
    ]
    loads[0].start()

    barrier = pltpu.get_barrier_semaphore()
    friends = [at(x, y, 1 - core)] + [along_x(k) for k in range(1, nx)]
    friends += [along_y(k) for k in near(ny)] + [along_z(k) for k in near(n_col)]
    for friend in friends:
        pl.semaphore_signal(barrier, inc=1, device_id=friend, device_id_type=MESH)

    for load in loads[1:]:
        load.start()
    loads[0].wait()

    per = width // 128
    u = users_ref[...]
    gram = dot(u, u, TN)
    for a in range(width // 8):
        for h in range(per):
            local[a * per + h] = gram[8 * a:8 * a + 8, 128 * h:128 * h + 128]

    pl.semaphore_wait(barrier, len(friends))

    def meet(semaphores, i, n, along):
        for k in (rounds(n)[i], n - rounds(n)[i]):
            pl.semaphore_signal(semaphores.at[i], inc=1, device_id=along(k), device_id_type=MESH)

    def met(semaphores, i):
        pl.semaphore_wait(semaphores.at[i], 2)

    def send(index, source, target, device):
        pltpu.make_async_remote_copy(
            src_ref=source, dst_ref=target, send_sem=send_sems.at[index], recv_sem=recv_sems.at[index],
            device_id=device, device_id_type=MESH,
        ).start()

    def wait(view, sem):
        pltpu.make_async_copy(view, view, sem).wait()

    def arrived(index, view):
        wait(view, recv_sems.at[index])

    def total(buffer, count):
        value = buffer[0]
        for k in range(1, count):
            value = value + buffer[k]
        return value

    def send_rows(steps):
        side = 2 * nx
        for step in steps:
            def one(k, carry):
                peer = lax.rem(y + step, ny) * side + lax.rem(lax.rem(r, side) + k, side)
                pltpu.make_async_remote_copy(
                    src_ref=outgoing.at[peer], dst_ref=recv.at[r], send_sem=row_send, recv_sem=row_recv,
                    device_id=(peer, c), device_id_type=MESH,
                ).start()
                return carry

            lax.fori_loop(0 if step else 1, side, one, 0)

    first, second = parted(ny)

    half_tiles = s0.shape[0]
    send(0, local.at[pl.ds((1 - core) * half_tiles, half_tiles)], s0, at(x, y, 1 - core))
    if rounds(ny):
        meet(met_y, 0, ny, along_y)
    if rounds(n_col):
        meet(met_z, 0, n_col, along_z)
    arrived(0, s0)
    p0[...] = local[pl.ds(core * half_tiles, half_tiles)] + s0[...]

    tiles_x = s1.shape[1]
    for k in far_first(nx):
        px = lax.rem(x + k, nx)
        send(1, p0.at[pl.ds(px * tiles_x, tiles_x)], s1.at[x], along_x(k))
    s1[x] = p0[pl.ds(x * tiles_x, tiles_x)]
    for i in range(1, len(rounds(n_col))):
        met(met_z, i - 1)
        meet(met_z, i, n_col, along_z)
    arrived(1, s1.at[pl.ds(0, nx - 1)])
    p1[...] = total(s1, nx)

    if rounds(ny):
        met(met_y, 0)
    tiles_y = s2.shape[1]
    for k in far_first(ny):
        py = lax.rem(y + k, ny)
        send(2, p1.at[pl.ds(py * tiles_y, tiles_y)], s2.at[y], along_y(k))
    s2[y] = p1[pl.ds(y * tiles_y, tiles_y)]
    loads[1].wait()
    wanted = wanted_ref[...].T[:, :, None]
    pick = (wanted == lax.broadcasted_iota(jnp.int32, (n_row, slots, rows_dev), 2)).astype(F32)
    rows_out = dot(pick.reshape(n_recv, rows_dev).astype(BF16), u).astype(BF16)
    outgoing[...] = rows_out.reshape(n_row, slots, width)
    recv[r] = outgoing[r]
    send_rows([0])
    arrived(2, s2.at[pl.ds(0, ny - 1)])
    p2[...] = total(s2, ny)

    if rounds(n_col):
        met(met_z, len(rounds(n_col)) - 1)
    for k in far_first(n_col):
        send(3, p2, s3.at[c], along_z(k))
    s3[c] = p2[...]
    send_rows(first)

    for load in loads[2:]:
        load.wait()
    tiles = tile_users_ref.shape[0]
    block = tile_users_ref.shape[1]
    blocks = items_ref.shape[0] // block
    items = blocks * block
    live = live_ref[0]
    for t in range(tiles):
        columns = slice(t * block, (t + 1) * block)
        hit = lax.broadcasted_iota(jnp.int32, (n_recv, block), 0) == tile_users_ref[t:t + 1, :]
        hot[:, columns] = hit.astype(F32).astype(BF16)
        counts = counts_ref[t].astype(F32)
        pref = (counts > 0).astype(F32)
        alive = (t < live).astype(F32)
        for k in range(blocks):
            mine = (tile_block_ref[t] == k).astype(F32) * alive
            left[k * block:(k + 1) * block, columns] = (counts * mine).astype(BF16)
            left[items + k * block:items + (k + 1) * block, columns] = (pref * mine).astype(BF16)
    sums = dot(left[...], hot[...], NT)
    conf_all = 40.0 * sums[:items]
    conf[...] = conf_all
    high, low = split(sums[items:] + conf_all)
    rh[...] = high
    rl[...] = low

    arrived(3, s3.at[pl.ds(0, n_col - 1)])
    here = pl.ds(y * tiles_y, tiles_y)
    s4[here] = total(s3, n_col)

    for k in far_first(ny):
        send(4, s4.at[here], s4.at[here], along_y(k))
    send_rows(second)
    arrived(4, s4.at[pl.ds(0, (ny - 1) * tiles_y)])

    mine = pl.ds((core * nx + x) * tiles_x, tiles_x)
    for k in far_first(nx):
        for other in (core, 1 - core):
            send(5, s4, full.at[mine], at(lax.rem(x + k, nx), y, other))
    send(5, s4, full.at[mine], at(x, y, 1 - core))
    full[mine] = s4[...]

    wait(recv.at[pl.ds(0, n_row - 1)], row_recv)

    rows = recv[...].reshape(n_recv, width)

    def pieces():
        step = n_recv // CHUNKS
        return [slice(k * step, (k + 1) * step) for k in range(CHUNKS)]

    def tile_part(parts):
        image = None
        for piece in pieces():
            some = rows[piece]
            share = dot_stacked(stacked(conf[:, piece] * dot_stacked(parts, some, NT)), some)
            image = share if image is None else image + share
        return image

    def tile_curve(parts):
        curve = None
        for piece in pieces():
            share = jnp.sum(conf[:, piece] * jnp.square(dot_stacked(parts, rows[piece], NT)), axis=1, keepdims=True)
            curve = share if curve is None else curve + share
        return curve

    start = items_ref[...]
    parts = stacked(start)
    resid = dot(rh[...], rows) + dot(rl[...], rows) - tile_part(parts) - 0.1 * start

    arrived(5, full.at[pl.ds(0, (2 * nx - 1) * tiles_x)])
    strips = []
    for a in range(width // 8):
        strips.append(jnp.concatenate([full[a * per + h] for h in range(per)], axis=1))
    gh, gl = split(jnp.concatenate(strips, axis=0))

    def gram_part(parts):
        return dot_stacked(parts, gh) + dot(parts[:items], gl)

    resid = resid - gram_part(parts)
    solution = start
    direction = resid
    norm_now = jnp.sum(resid * resid, axis=1, keepdims=True)
    for step in range(ITERS):
        parts = stacked(direction)
        image = gram_part(parts) + 0.1 * direction
        if step == ITERS - 1:
            curve = jnp.sum(direction * image, axis=1, keepdims=True)
            curve = curve + tile_curve(parts)
            out_ref[...] = solution + norm_now / curve * direction
            break
        image = image + tile_part(parts)
        alpha = norm_now / jnp.sum(direction * image, axis=1, keepdims=True)
        solution = solution + alpha * direction
        resid = resid - alpha * image
        norm_next = jnp.sum(resid * resid, axis=1, keepdims=True)
        direction = resid + norm_next / norm_now * direction
        norm_now = norm_next

    wait(outgoing.at[pl.ds(0, n_row - 1)], row_send)
    sent = [s0, s1.at[pl.ds(0, nx - 1)], s2.at[pl.ds(0, ny - 1)], s3.at[pl.ds(0, n_col - 1)],
            s4.at[pl.ds(0, (ny - 1) * tiles_y)]]
    sent += [full.at[pl.ds(0, (2 * nx - 1) * tiles_x)]]
    for index, view in enumerate(sent):
        wait(view, send_sems.at[index])

def body(dims, user_factors, item_factors, send_rows, tile_users, tile_block, tile_counts, tile_live):
    ny, nx, n_col = dims
    n_row = ny * nx * 2
    width = user_factors.shape[1]
    slots = send_rows.shape[1]
    n_tiles = width // 8 * (width // 128)
    tiles_x = n_tiles // 2 // nx
    tiles_y = tiles_x // ny
    n_recv = n_row * slots
    columns = tile_users.shape[0] * tile_users.shape[1]
    items = item_factors.shape[0]
    operands = (user_factors, item_factors, send_rows.T, tile_users, tile_block, tile_counts, tile_live.reshape(1))
    places = (pltpu.VMEM, pltpu.VMEM, pltpu.VMEM, pltpu.VMEM, pltpu.SMEM, pltpu.VMEM, pltpu.SMEM)

    def cells(*lead):
        return pltpu.VMEM((*lead, 8, 128), F32)

    return pl.pallas_call(
        functools.partial(kernel, dims),
        out_shape=pltpu.VMEM(item_factors.shape, F32),
        in_specs=[pl.BlockSpec(memory_space=pltpu.HBM)] * len(operands),
        out_specs=pl.BlockSpec(memory_space=pltpu.VMEM),
        scratch_shapes=[place(a.shape, a.dtype) for place, a in zip(places, operands)] + [
            pltpu.VMEM((n_row, slots, width), BF16),
            pltpu.VMEM((n_row, slots, width), BF16),
            cells(n_tiles),
            cells(n_tiles // 2),
            cells(n_tiles // 2),
            cells(nx, tiles_x),
            cells(tiles_x),
            cells(ny, tiles_y),
            cells(tiles_y),
            cells(n_col, tiles_y),
            cells(tiles_x),
            cells(n_tiles),
            pltpu.VMEM((n_recv, columns), BF16),
            pltpu.VMEM((2 * items, columns), BF16),
            pltpu.VMEM((items, n_recv), F32),
            pltpu.VMEM((items, n_recv), BF16),
            pltpu.VMEM((items, n_recv), BF16),
            pltpu.SemaphoreType.DMA((len(operands),)),
            pltpu.SemaphoreType.DMA,
            pltpu.SemaphoreType.DMA,
            pltpu.SemaphoreType.DMA((7,)),
            pltpu.SemaphoreType.DMA((7,)),
            pltpu.SemaphoreType.REGULAR((max(1, len(rounds(ny))),)),
            pltpu.SemaphoreType.REGULAR((max(1, len(rounds(n_col))),)),
        ],
        compiler_params=pltpu.CompilerParams(
            collective_id=0, has_side_effects=True, vmem_limit_bytes=58 * 1024 * 1024
        ),
    )(*operands)


def solution(mesh):
    n_row, n_col = mesh.shape["row"], mesh.shape["col"]
    nx = min(4, n_row // 4)
    in_specs = (
        P(("row", "col"), None),
        P(("row", "col"), None),
        P(("row", "col"), None),
        P(("row", "col"), None),
        P(("row", "col")),
        P(("row", "col"), None, None),
        P("row", "col"),
    )
    return jax.shard_map(
        functools.partial(body, (n_row // 2 // nx, nx, n_col)),
        mesh=mesh, in_specs=in_specs, out_specs=P(("row", "col"), None), check_vma=False,
    )
```

```python
import functools

import jax
import jax.numpy as jnp
from jax import lax
from jax.experimental import pallas as pl
from jax.experimental.pallas import tpu as pltpu
from jax.sharding import PartitionSpec as P

ITERS = 3
FIRST = (5, 4, 3, 1)
CHUNKS = 4
MESH = pl.DeviceIdType.MESH
F32 = jnp.float32
BF16 = jnp.bfloat16

NN = (((1,), (0,)), ((), ()))
NT = (((1,), (1,)), ((), ()))
TN = (((0,), (0,)), ((), ()))


def dot(a, b, dims=NN):
    return lax.dot_general(a, b, dims, preferred_element_type=F32)


def split(x):
    high = x.astype(BF16)
    return high, (x - high.astype(F32)).astype(BF16)


def stacked(x):
    return jnp.concatenate(split(x), axis=0)


def dot_stacked(parts, b, dims=NN):
    both = dot(parts, b, dims)
    half = both.shape[0] // 2
    return both[:half] + both[half:]


def far_first(n):
    return sorted(range(1, n), key=lambda k: -min(k, n - k))


def near(n):
    return sorted({k % n for k in (2, -2, 1, -1)} - {0})


def parted(n):
    first = [k for k in FIRST if k < n]
    return first, [k for k in far_first(n) if k not in first]


def rounds(n):
    known, steps = 2, []
    while known < n // 2:
        steps.append(known)
        known *= 2
    return steps


def kernel(
    dims,
    users_hbm, items_hbm, wanted_hbm, tile_users_hbm, tile_block_hbm, counts_hbm, live_hbm,
    out_ref,
    users_ref, items_ref, wanted_ref, tile_users_ref, tile_block_ref, counts_ref, live_ref,
    outgoing, recv, local, s0, p0, s1, p1, s2, p2, s3, s4, full, hot, left, conf, rh, rl,
    load_sems, row_send, row_recv, send_sems, recv_sems, met_y, met_z,
):
    ny, nx, n_col = dims
    n_row = ny * nx * 2
    r = lax.axis_index("row")
    c = lax.axis_index("col")
    core = lax.rem(r, 2)
    x = lax.rem(lax.div(r, 2), nx)
    y = lax.div(r, 2 * nx)
    rows_dev, width = users_ref.shape
    slots = wanted_ref.shape[0]
    n_recv = n_row * slots

    def at(px, py, pcore):
        return ((py * nx + px) * 2 + pcore, c)

    def along_x(k):
        return at(lax.rem(x + k, nx), y, core)

    def along_y(k):
        return at(x, lax.rem(y + k, ny), core)

    def along_z(k):
        return (r, lax.rem(c + k, n_col))

    loads = [
        pltpu.make_async_copy(source, target, load_sems.at[i])
        for i, (source, target) in enumerate((
            (users_hbm, users_ref), (wanted_hbm, wanted_ref), (items_hbm, items_ref), (tile_users_hbm, tile_users_ref),
            (tile_block_hbm, tile_block_ref), (live_hbm, live_ref), (counts_hbm, counts_ref),
        ))
    ]
    loads[0].start()

    barrier = pltpu.get_barrier_semaphore()
    friends = [at(x, y, 1 - core)] + [along_x(k) for k in range(1, nx)]
    friends += [along_y(k) for k in near(ny)] + [along_z(k) for k in near(n_col)]
    for friend in friends:
        pl.semaphore_signal(barrier, inc=1, device_id=friend, device_id_type=MESH)

    for load in loads[1:]:
        load.start()
    loads[0].wait()

    per = width // 128
    u = users_ref[...]
    gram = dot(u, u, TN)
    for a in range(width // 8):
        for h in range(per):
            local[a * per + h] = gram[8 * a:8 * a + 8, 128 * h:128 * h + 128]

    pl.semaphore_wait(barrier, len(friends))

    def meet(semaphores, i, n, along):
        for k in (rounds(n)[i], n - rounds(n)[i]):
            pl.semaphore_signal(semaphores.at[i], inc=1, device_id=along(k), device_id_type=MESH)

    def met(semaphores, i):
        pl.semaphore_wait(semaphores.at[i], 2)

    def send(index, source, target, device):
        pltpu.make_async_remote_copy(
            src_ref=source, dst_ref=target, send_sem=send_sems.at[index], recv_sem=recv_sems.at[index],
            device_id=device, device_id_type=MESH,
        ).start()

    def wait(view, sem):
        pltpu.make_async_copy(view, view, sem).wait()

    def arrived(index, view):
        wait(view, recv_sems.at[index])

    def total(buffer, count):
        value = buffer[0]
        for k in range(1, count):
            value = value + buffer[k]
        return value

    def send_rows(steps):
        side = 2 * nx
        j = lax.rem(r, side)

        def one(k, carry):
            for step in steps:
                peer = lax.rem(y + step, ny) * side + lax.rem(j + k, side)
                pltpu.make_async_remote_copy(
                    src_ref=outgoing.at[peer], dst_ref=recv.at[r], send_sem=row_send, recv_sem=row_recv,
                    device_id=(peer, c), device_id_type=MESH,
                ).start()
            return carry

        if steps:
            lax.fori_loop(1 if 0 in steps else 0, side, one, 0)

    first, second = parted(ny)

    half_tiles = s0.shape[0]
    send(0, local.at[pl.ds((1 - core) * half_tiles, half_tiles)], s0, at(x, y, 1 - core))
    if rounds(ny):
        meet(met_y, 0, ny, along_y)
    if rounds(n_col):
        meet(met_z, 0, n_col, along_z)
    arrived(0, s0)
    p0[...] = local[pl.ds(core * half_tiles, half_tiles)] + s0[...]

    tiles_x = s1.shape[1]
    for k in far_first(nx):
        px = lax.rem(x + k, nx)
        send(1, p0.at[pl.ds(px * tiles_x, tiles_x)], s1.at[x], along_x(k))
    s1[x] = p0[pl.ds(x * tiles_x, tiles_x)]
    for i in range(1, len(rounds(n_col))):
        met(met_z, i - 1)
        meet(met_z, i, n_col, along_z)
    arrived(1, s1.at[pl.ds(0, nx - 1)])
    p1[...] = total(s1, nx)

    if rounds(ny):
        met(met_y, 0)
    tiles_y = s2.shape[1]
    for k in far_first(ny):
        py = lax.rem(y + k, ny)
        send(2, p1.at[pl.ds(py * tiles_y, tiles_y)], s2.at[y], along_y(k))
    s2[y] = p1[pl.ds(y * tiles_y, tiles_y)]
    loads[1].wait()
    wanted = wanted_ref[...].T[:, :, None]
    pick = (wanted == lax.broadcasted_iota(jnp.int32, (n_row, slots, rows_dev), 2)).astype(F32)
    rows_out = dot(pick.reshape(n_recv, rows_dev).astype(BF16), u).astype(BF16)
    outgoing[...] = rows_out.reshape(n_row, slots, width)
    recv[r] = outgoing[r]
    send_rows([0])
    arrived(2, s2.at[pl.ds(0, ny - 1)])
    p2[...] = total(s2, ny)

    if rounds(n_col):
        met(met_z, len(rounds(n_col)) - 1)
    for k in far_first(n_col):
        send(3, p2, s3.at[c], along_z(k))
    s3[c] = p2[...]
    send_rows(first)

    for load in loads[2:]:
        load.wait()
    tiles = tile_users_ref.shape[0]
    block = tile_users_ref.shape[1]
    blocks = items_ref.shape[0] // block
    items = blocks * block
    live = live_ref[0]
    for t in range(tiles):
        columns = slice(t * block, (t + 1) * block)
        hit = lax.broadcasted_iota(jnp.int32, (n_recv, block), 0) == tile_users_ref[t:t + 1, :]
        hot[:, columns] = hit.astype(F32).astype(BF16)
        counts = counts_ref[t].astype(F32)
        pref = (counts > 0).astype(F32)
        alive = (t < live).astype(F32)
        for k in range(blocks):
            mine = (tile_block_ref[t] == k).astype(F32) * alive
            left[k * block:(k + 1) * block, columns] = (counts * mine).astype(BF16)
            left[items + k * block:items + (k + 1) * block, columns] = (pref * mine).astype(BF16)
    sums = dot(left[...], hot[...], NT)
    conf_all = 40.0 * sums[:items]
    conf[...] = conf_all
    high, low = split(sums[items:] + conf_all)
    rh[...] = high
    rl[...] = low

    arrived(3, s3.at[pl.ds(0, n_col - 1)])
    here = pl.ds(y * tiles_y, tiles_y)
    s4[here] = total(s3, n_col)

    for k in far_first(ny):
        send(4, s4.at[here], s4.at[here], along_y(k))
    send_rows(second)
    arrived(4, s4.at[pl.ds(0, (ny - 1) * tiles_y)])

    mine = pl.ds((core * nx + x) * tiles_x, tiles_x)
    for k in far_first(nx):
        for other in (core, 1 - core):
            send(5, s4, full.at[mine], at(lax.rem(x + k, nx), y, other))
    send(5, s4, full.at[mine], at(x, y, 1 - core))
    full[mine] = s4[...]

    wait(recv.at[pl.ds(0, n_row - 1)], row_recv)

    rows = recv[...].reshape(n_recv, width)

    def pieces():
        step = n_recv // CHUNKS
        return [slice(k * step, (k + 1) * step) for k in range(CHUNKS)]

    def tile_part(parts):
        image = None
        for piece in pieces():
            some = rows[piece]
            share = dot_stacked(stacked(conf[:, piece] * dot_stacked(parts, some, NT)), some)
            image = share if image is None else image + share
        return image

    def tile_curve(parts):
        curve = None
        for piece in pieces():
            share = jnp.sum(conf[:, piece] * jnp.square(dot_stacked(parts, rows[piece], NT)), axis=1, keepdims=True)
            curve = share if curve is None else curve + share
        return curve

    start = items_ref[...]
    parts = stacked(start)
    resid = dot(rh[...], rows) + dot(rl[...], rows) - tile_part(parts) - 0.1 * start

    arrived(5, full.at[pl.ds(0, (2 * nx - 1) * tiles_x)])
    strips = []
    for a in range(width // 8):
        strips.append(jnp.concatenate([full[a * per + h] for h in range(per)], axis=1))
    gh, gl = split(jnp.concatenate(strips, axis=0))

    def gram_part(parts):
        return dot_stacked(parts, gh) + dot(parts[:items], gl)

    resid = resid - gram_part(parts)
    solution = start
    direction = resid
    norm_now = jnp.sum(resid * resid, axis=1, keepdims=True)
    for step in range(ITERS):
        parts = stacked(direction)
        image = gram_part(parts) + 0.1 * direction
        if step == ITERS - 1:
            curve = jnp.sum(direction * image, axis=1, keepdims=True)
            curve = curve + tile_curve(parts)
            out_ref[...] = solution + norm_now / curve * direction
            break
        image = image + tile_part(parts)
        alpha = norm_now / jnp.sum(direction * image, axis=1, keepdims=True)
        solution = solution + alpha * direction
        resid = resid - alpha * image
        norm_next = jnp.sum(resid * resid, axis=1, keepdims=True)
        direction = resid + norm_next / norm_now * direction
        norm_now = norm_next

    wait(outgoing.at[pl.ds(0, n_row - 1)], row_send)
    sent = [s0, s1.at[pl.ds(0, nx - 1)], s2.at[pl.ds(0, ny - 1)], s3.at[pl.ds(0, n_col - 1)],
            s4.at[pl.ds(0, (ny - 1) * tiles_y)]]
    sent += [full.at[pl.ds(0, (2 * nx - 1) * tiles_x)]]
    for index, view in enumerate(sent):
        wait(view, send_sems.at[index])

def body(dims, user_factors, item_factors, send_rows, tile_users, tile_block, tile_counts, tile_live):
    ny, nx, n_col = dims
    n_row = ny * nx * 2
    width = user_factors.shape[1]
    slots = send_rows.shape[1]
    n_tiles = width // 8 * (width // 128)
    tiles_x = n_tiles // 2 // nx
    tiles_y = tiles_x // ny
    n_recv = n_row * slots
    columns = tile_users.shape[0] * tile_users.shape[1]
    items = item_factors.shape[0]
    operands = (user_factors, item_factors, send_rows.T, tile_users, tile_block, tile_counts, tile_live.reshape(1))
    places = (pltpu.VMEM, pltpu.VMEM, pltpu.VMEM, pltpu.VMEM, pltpu.SMEM, pltpu.VMEM, pltpu.SMEM)

    def cells(*lead):
        return pltpu.VMEM((*lead, 8, 128), F32)

    return pl.pallas_call(
        functools.partial(kernel, dims),
        out_shape=pltpu.VMEM(item_factors.shape, F32),
        in_specs=[pl.BlockSpec(memory_space=pltpu.HBM)] * len(operands),
        out_specs=pl.BlockSpec(memory_space=pltpu.VMEM),
        scratch_shapes=[place(a.shape, a.dtype) for place, a in zip(places, operands)] + [
            pltpu.VMEM((n_row, slots, width), BF16),
            pltpu.VMEM((n_row, slots, width), BF16),
            cells(n_tiles),
            cells(n_tiles // 2),
            cells(n_tiles // 2),
            cells(nx, tiles_x),
            cells(tiles_x),
            cells(ny, tiles_y),
            cells(tiles_y),
            cells(n_col, tiles_y),
            cells(tiles_x),
            cells(n_tiles),
            pltpu.VMEM((n_recv, columns), BF16),
            pltpu.VMEM((2 * items, columns), BF16),
            pltpu.VMEM((items, n_recv), F32),
            pltpu.VMEM((items, n_recv), BF16),
            pltpu.VMEM((items, n_recv), BF16),
            pltpu.SemaphoreType.DMA((len(operands),)),
            pltpu.SemaphoreType.DMA,
            pltpu.SemaphoreType.DMA,
            pltpu.SemaphoreType.DMA((7,)),
            pltpu.SemaphoreType.DMA((7,)),
            pltpu.SemaphoreType.REGULAR((max(1, len(rounds(ny))),)),
            pltpu.SemaphoreType.REGULAR((max(1, len(rounds(n_col))),)),
        ],
        compiler_params=pltpu.CompilerParams(
            collective_id=0, has_side_effects=True, vmem_limit_bytes=58 * 1024 * 1024
        ),
    )(*operands)


def solution(mesh):
    n_row, n_col = mesh.shape["row"], mesh.shape["col"]
    nx = min(4, n_row // 4)
    in_specs = (
        P(("row", "col"), None),
        P(("row", "col"), None),
        P(("row", "col"), None),
        P(("row", "col"), None),
        P(("row", "col")),
        P(("row", "col"), None, None),
        P("row", "col"),
    )
    return jax.shard_map(
        functools.partial(body, (n_row // 2 // nx, nx, n_col)),
        mesh=mesh, in_specs=in_specs, out_specs=P(("row", "col"), None), check_vma=False,
    )
```

```python
import functools

import jax
import jax.numpy as jnp
from jax import lax
from jax.experimental import pallas as pl
from jax.experimental.pallas import tpu as pltpu
from jax.sharding import PartitionSpec as P

ITERS = 3
FIRST = (5, 4, 3, 1)
CHUNKS = 4
MESH = pl.DeviceIdType.MESH
F32 = jnp.float32
BF16 = jnp.bfloat16

NN = (((1,), (0,)), ((), ()))
NT = (((1,), (1,)), ((), ()))
TN = (((0,), (0,)), ((), ()))


def dot(a, b, dims=NN):
    return lax.dot_general(a, b, dims, preferred_element_type=F32)


def split(x):
    high = x.astype(BF16)
    return high, (x - high.astype(F32)).astype(BF16)


def stacked(x):
    return jnp.concatenate(split(x), axis=0)


def dot_stacked(parts, b, dims=NN):
    both = dot(parts, b, dims)
    half = both.shape[0] // 2
    return both[:half] + both[half:]


def far_first(n):
    return sorted(range(1, n), key=lambda k: -min(k, n - k))


def near(n, reach=2):
    return sorted({k % n for k in range(-reach, reach + 1)} - {0})


def parted(n):
    first = [k for k in FIRST if k < n]
    return first, [k for k in far_first(n) if k not in first]


def rounds(n, known=2):
    steps = []
    while known < n // 2:
        steps.append(known)
        known *= 2
    return steps


def kernel(
    dims,
    users_hbm, items_hbm, wanted_hbm, tile_users_hbm, tile_block_hbm, counts_hbm, live_hbm,
    out_ref,
    users_ref, items_ref, wanted_ref, tile_users_ref, tile_block_ref, counts_ref, live_ref,
    outgoing, recv, local, s0, p0, s1, p1, s2, p2, s3, s4, full, hot, left, conf, rh, rl,
    load_sems, row_send, row_recv, send_sems, recv_sems, met_y, met_z,
):
    ny, nx, n_col = dims
    n_row = ny * nx * 2
    r = lax.axis_index("row")
    c = lax.axis_index("col")
    core = lax.rem(r, 2)
    x = lax.rem(lax.div(r, 2), nx)
    y = lax.div(r, 2 * nx)
    rows_dev, width = users_ref.shape
    slots = wanted_ref.shape[0]
    n_recv = n_row * slots

    def at(px, py, pcore):
        return ((py * nx + px) * 2 + pcore, c)

    def along_x(k):
        return at(lax.rem(x + k, nx), y, core)

    def along_y(k):
        return at(x, lax.rem(y + k, ny), core)

    def along_z(k):
        return (r, lax.rem(c + k, n_col))

    loads = [
        pltpu.make_async_copy(source, target, load_sems.at[i])
        for i, (source, target) in enumerate((
            (users_hbm, users_ref), (wanted_hbm, wanted_ref), (items_hbm, items_ref), (tile_users_hbm, tile_users_ref),
            (tile_block_hbm, tile_block_ref), (live_hbm, live_ref), (counts_hbm, counts_ref),
        ))
    ]
    loads[0].start()

    barrier = pltpu.get_barrier_semaphore()
    friends = [at(x, y, 1 - core)] + [along_x(k) for k in range(1, nx)]
    friends += [along_y(k) for k in near(ny)] + [along_z(k) for k in near(n_col, 4)]
    for friend in friends:
        pl.semaphore_signal(barrier, inc=1, device_id=friend, device_id_type=MESH)

    for load in loads[1:]:
        load.start()
    loads[0].wait()

    per = width // 128
    u = users_ref[...]
    gram = dot(u, u, TN)
    for a in range(width // 8):
        for h in range(per):
            local[a * per + h] = gram[8 * a:8 * a + 8, 128 * h:128 * h + 128]

    pl.semaphore_wait(barrier, len(friends))

    def meet(semaphores, i, n, along):
        for k in (rounds(n, 2 if n == ny else 4)[i], n - rounds(n, 2 if n == ny else 4)[i]):
            pl.semaphore_signal(semaphores.at[i], inc=1, device_id=along(k), device_id_type=MESH)

    def met(semaphores, i):
        pl.semaphore_wait(semaphores.at[i], 2)

    def send(index, source, target, device):
        pltpu.make_async_remote_copy(
            src_ref=source, dst_ref=target, send_sem=send_sems.at[index], recv_sem=recv_sems.at[index],
            device_id=device, device_id_type=MESH,
        ).start()

    def wait(view, sem):
        pltpu.make_async_copy(view, view, sem).wait()

    def arrived(index, view):
        wait(view, recv_sems.at[index])

    def total(buffer, count):
        value = buffer[0]
        for k in range(1, count):
            value = value + buffer[k]
        return value

    def send_rows(steps):
        side = 2 * nx
        j = lax.rem(r, side)

        def one(k, carry):
            for step in steps:
                peer = lax.rem(y + step, ny) * side + lax.rem(j + k, side)
                pltpu.make_async_remote_copy(
                    src_ref=outgoing.at[peer], dst_ref=recv.at[r], send_sem=row_send, recv_sem=row_recv,
                    device_id=(peer, c), device_id_type=MESH,
                ).start()
            return carry

        if steps:
            lax.fori_loop(1 if 0 in steps else 0, side, one, 0)

    first, second = parted(ny)

    half_tiles = s0.shape[0]
    send(0, local.at[pl.ds((1 - core) * half_tiles, half_tiles)], s0, at(x, y, 1 - core))
    if rounds(ny):
        meet(met_y, 0, ny, along_y)
    if rounds(n_col, 4):
        meet(met_z, 0, n_col, along_z)
    arrived(0, s0)
    p0[...] = local[pl.ds(core * half_tiles, half_tiles)] + s0[...]

    tiles_x = s1.shape[1]
    for k in far_first(nx):
        px = lax.rem(x + k, nx)
        send(1, p0.at[pl.ds(px * tiles_x, tiles_x)], s1.at[x], along_x(k))
    s1[x] = p0[pl.ds(x * tiles_x, tiles_x)]
    for i in range(1, len(rounds(n_col, 4))):
        met(met_z, i - 1)
        meet(met_z, i, n_col, along_z)
    arrived(1, s1.at[pl.ds(0, nx - 1)])
    p1[...] = total(s1, nx)

    if rounds(ny):
        met(met_y, 0)
    tiles_y = s2.shape[1]
    for k in far_first(ny):
        py = lax.rem(y + k, ny)
        send(2, p1.at[pl.ds(py * tiles_y, tiles_y)], s2.at[y], along_y(k))
    s2[y] = p1[pl.ds(y * tiles_y, tiles_y)]
    loads[1].wait()
    wanted = wanted_ref[...].T[:, :, None]
    pick = (wanted == lax.broadcasted_iota(jnp.int32, (n_row, slots, rows_dev), 2)).astype(F32)
    rows_out = dot(pick.reshape(n_recv, rows_dev).astype(BF16), u).astype(BF16)
    outgoing[...] = rows_out.reshape(n_row, slots, width)
    recv[r] = outgoing[r]
    send_rows([0])
    arrived(2, s2.at[pl.ds(0, ny - 1)])
    p2[...] = total(s2, ny)

    if rounds(n_col, 4):
        met(met_z, len(rounds(n_col, 4)) - 1)
    for k in far_first(n_col):
        send(3, p2, s3.at[c], along_z(k))
    s3[c] = p2[...]
    send_rows(first)

    for load in loads[2:]:
        load.wait()
    tiles = tile_users_ref.shape[0]
    block = tile_users_ref.shape[1]
    blocks = items_ref.shape[0] // block
    items = blocks * block
    live = live_ref[0]
    for t in range(tiles):
        columns = slice(t * block, (t + 1) * block)
        hit = lax.broadcasted_iota(jnp.int32, (n_recv, block), 0) == tile_users_ref[t:t + 1, :]
        hot[:, columns] = hit.astype(F32).astype(BF16)
        counts = counts_ref[t].astype(F32)
        pref = (counts > 0).astype(F32)
        alive = (t < live).astype(F32)
        for k in range(blocks):
            mine = (tile_block_ref[t] == k).astype(F32) * alive
            left[k * block:(k + 1) * block, columns] = (counts * mine).astype(BF16)
            left[items + k * block:items + (k + 1) * block, columns] = (pref * mine).astype(BF16)
    sums = dot(left[...], hot[...], NT)
    conf_all = 40.0 * sums[:items]
    conf[...] = conf_all
    high, low = split(sums[items:] + conf_all)
    rh[...] = high
    rl[...] = low

    arrived(3, s3.at[pl.ds(0, n_col - 1)])
    here = pl.ds(y * tiles_y, tiles_y)
    s4[here] = total(s3, n_col)

    for k in far_first(ny):
        send(4, s4.at[here], s4.at[here], along_y(k))
    send_rows(second)
    arrived(4, s4.at[pl.ds(0, (ny - 1) * tiles_y)])

    mine = pl.ds((core * nx + x) * tiles_x, tiles_x)
    for k in far_first(nx):
        for other in (core, 1 - core):
            send(5, s4, full.at[mine], at(lax.rem(x + k, nx), y, other))
    send(5, s4, full.at[mine], at(x, y, 1 - core))
    full[mine] = s4[...]

    wait(recv.at[pl.ds(0, n_row - 1)], row_recv)

    rows = recv[...].reshape(n_recv, width)

    def pieces():
        step = n_recv // CHUNKS
        return [slice(k * step, (k + 1) * step) for k in range(CHUNKS)]

    def tile_part(parts):
        image = None
        for piece in pieces():
            some = rows[piece]
            share = dot_stacked(stacked(conf[:, piece] * dot_stacked(parts, some, NT)), some)
            image = share if image is None else image + share
        return image

    def tile_curve(parts):
        curve = None
        for piece in pieces():
            share = jnp.sum(conf[:, piece] * jnp.square(dot_stacked(parts, rows[piece], NT)), axis=1, keepdims=True)
            curve = share if curve is None else curve + share
        return curve

    start = items_ref[...]
    parts = stacked(start)
    resid = dot(rh[...], rows) + dot(rl[...], rows) - tile_part(parts) - 0.1 * start

    arrived(5, full.at[pl.ds(0, (2 * nx - 1) * tiles_x)])
    strips = []
    for a in range(width // 8):
        strips.append(jnp.concatenate([full[a * per + h] for h in range(per)], axis=1))
    gh, gl = split(jnp.concatenate(strips, axis=0))

    def gram_part(parts):
        return dot_stacked(parts, gh) + dot(parts[:items], gl)

    resid = resid - gram_part(parts)
    solution = start
    direction = resid
    norm_now = jnp.sum(resid * resid, axis=1, keepdims=True)
    for step in range(ITERS):
        parts = stacked(direction)
        image = gram_part(parts) + 0.1 * direction
        if step == ITERS - 1:
            curve = jnp.sum(direction * image, axis=1, keepdims=True)
            curve = curve + tile_curve(parts)
            out_ref[...] = solution + norm_now / curve * direction
            break
        image = image + tile_part(parts)
        alpha = norm_now / jnp.sum(direction * image, axis=1, keepdims=True)
        solution = solution + alpha * direction
        resid = resid - alpha * image
        norm_next = jnp.sum(resid * resid, axis=1, keepdims=True)
        direction = resid + norm_next / norm_now * direction
        norm_now = norm_next

    wait(outgoing.at[pl.ds(0, n_row - 1)], row_send)
    sent = [s0, s1.at[pl.ds(0, nx - 1)], s2.at[pl.ds(0, ny - 1)], s3.at[pl.ds(0, n_col - 1)],
            s4.at[pl.ds(0, (ny - 1) * tiles_y)]]
    sent += [full.at[pl.ds(0, (2 * nx - 1) * tiles_x)]]
    for index, view in enumerate(sent):
        wait(view, send_sems.at[index])

def body(dims, user_factors, item_factors, send_rows, tile_users, tile_block, tile_counts, tile_live):
    ny, nx, n_col = dims
    n_row = ny * nx * 2
    width = user_factors.shape[1]
    slots = send_rows.shape[1]
    n_tiles = width // 8 * (width // 128)
    tiles_x = n_tiles // 2 // nx
    tiles_y = tiles_x // ny
    n_recv = n_row * slots
    columns = tile_users.shape[0] * tile_users.shape[1]
    items = item_factors.shape[0]
    operands = (user_factors, item_factors, send_rows.T, tile_users, tile_block, tile_counts, tile_live.reshape(1))
    places = (pltpu.VMEM, pltpu.VMEM, pltpu.VMEM, pltpu.VMEM, pltpu.SMEM, pltpu.VMEM, pltpu.SMEM)

    def cells(*lead):
        return pltpu.VMEM((*lead, 8, 128), F32)

    return pl.pallas_call(
        functools.partial(kernel, dims),
        out_shape=pltpu.VMEM(item_factors.shape, F32),
        in_specs=[pl.BlockSpec(memory_space=pltpu.HBM)] * len(operands),
        out_specs=pl.BlockSpec(memory_space=pltpu.VMEM),
        scratch_shapes=[place(a.shape, a.dtype) for place, a in zip(places, operands)] + [
            pltpu.VMEM((n_row, slots, width), BF16),
            pltpu.VMEM((n_row, slots, width), BF16),
            cells(n_tiles),
            cells(n_tiles // 2),
            cells(n_tiles // 2),
            cells(nx, tiles_x),
            cells(tiles_x),
            cells(ny, tiles_y),
            cells(tiles_y),
            cells(n_col, tiles_y),
            cells(tiles_x),
            cells(n_tiles),
            pltpu.VMEM((n_recv, columns), BF16),
            pltpu.VMEM((2 * items, columns), BF16),
            pltpu.VMEM((items, n_recv), F32),
            pltpu.VMEM((items, n_recv), BF16),
            pltpu.VMEM((items, n_recv), BF16),
            pltpu.SemaphoreType.DMA((len(operands),)),
            pltpu.SemaphoreType.DMA,
            pltpu.SemaphoreType.DMA,
            pltpu.SemaphoreType.DMA((7,)),
            pltpu.SemaphoreType.DMA((7,)),
            pltpu.SemaphoreType.REGULAR((max(1, len(rounds(ny))),)),
            pltpu.SemaphoreType.REGULAR((max(1, len(rounds(n_col, 4))),)),
        ],
        compiler_params=pltpu.CompilerParams(
            collective_id=0, has_side_effects=True, vmem_limit_bytes=58 * 1024 * 1024
        ),
    )(*operands)


def solution(mesh):
    n_row, n_col = mesh.shape["row"], mesh.shape["col"]
    nx = min(4, n_row // 4)
    in_specs = (
        P(("row", "col"), None),
        P(("row", "col"), None),
        P(("row", "col"), None),
        P(("row", "col"), None),
        P(("row", "col")),
        P(("row", "col"), None, None),
        P("row", "col"),
    )
    return jax.shard_map(
        functools.partial(body, (n_row // 2 // nx, nx, n_col)),
        mesh=mesh, in_specs=in_specs, out_specs=P(("row", "col"), None), check_vma=False,
    )
```
